256 devices in a mesh: tm: 32 (over x, z_hi, core), rows: 8 (over y, z_lo).
Axes of the slice: x: 4, y: 4, z: 8 (z_hi: 4, z_lo: 2; z = z_hi * 2 + z_lo), core: 2. Of those that a mesh axis runs over, the one named last changes fastest.
Arguments:
- latents: bfloat16 [32, 64, 104, 384], P('tm', 'rows'), may hold values from -6 to 6
- norm_gain: float32 [384], replicated, may hold values from 0.1 to 1.9
- conv_weight: bfloat16 [3, 3, 3, 384, 384], replicated, may hold values from -0.0625 to 0.0625
- up_weight: bfloat16 [3, 384, 768], replicated, may hold values from -0.1875 to 0.1875
Outputs:
- upsampled: bfloat16 [64, 64, 104, 384], P('tm', 'rows')
The draws below stay inside these ranges and needn't reach their ends.
All inputs are finite; a program needn't handle non-finite values.
Results may differ from the reference program's by a relative error of at most 0.0052.
Values may be sent and summed in bfloat16 or wider, within the bound.
No kernel may reach another device: no remote copies, remote signals or barrier semaphores. Data moves between devices by JAX's collectives and lax.ppermute only.
A program may use at most 64 MiB of HBM per device.

```python
import jax
import jax.numpy as jnp
from jax import lax

C = 384
W = 104
H = 64
FRAMES = 32


def block_scale(rng, extent, pieces, low, largest):
    def one(position, parts):
        heights = jax.random.uniform(jax.random.fold_in(jax.random.fold_in(rng, 6), position), (parts,), jnp.float32, low / len(pieces), largest / len(pieces))
        return jnp.repeat(jnp.exp(heights), extent[position] // parts).reshape((-1,) + (1,) * (len(extent) - position - 1))

    loudness = one(*pieces[0])
    for cut in pieces[1:]:
        loudness = loudness * one(*cut)
    return loudness


def noise(stream_key, dims, deviation, bound, shards=(), dtype=jnp.bfloat16):
    level = block_scale(stream_key, dims, shards, -0.22, 0.18) if shards else 1.0
    drawn = jax.random.normal(stream_key, dims, jnp.float32) * deviation * level
    return jnp.minimum(jnp.maximum(drawn, -bound), bound).astype(dtype)


def setup_inputs(seed: int = 0) -> dict:
    seeds = jax.random.split(jax.random.key(seed), 5)
    return {
        "latents": noise(seeds[0], (FRAMES, H, W, C), 1.0, 6.0, ((0, 32), (1, 8))),
        "norm_gain": jnp.clip(1.0 + 0.18 * jax.random.normal(seeds[1], (C,), jnp.float32), 0.1, 1.9),
        "conv_weight": noise(seeds[2], (3, 3, 3, C, C), (27 * C) ** -0.5, 0.0625),
        "up_weight": noise(seeds[3], (3, C, 2 * C), (3 * C) ** -0.5, 0.1875),
    }


EPS = 1e-06

def convolve(inputs, kernel, padding):
    return lax.conv_general_dilated(inputs, kernel, (1, 1, 1), padding, dimension_numbers=('NDHWC', 'DHWIO', 'NDHWC'), preferred_element_type=jnp.float32)

def reference(latents, norm_gain, conv_weight, up_weight):
    values = latents.astype(jnp.float32)
    scaled = values * lax.rsqrt(lax.optimization_barrier(jnp.mean(values * values, axis=-1, keepdims=True)) + EPS) * norm_gain
    activated = jax.nn.silu(scaled).astype(jnp.bfloat16)
    convolved = convolve(activated[None], conv_weight, ((2, 0), (1, 1), (1, 1)))[0]
    block_out = (values + convolved).astype(jnp.bfloat16)
    doubled = convolve(block_out[None], up_weight[:, None, None], ((2, 0), (0, 0), (0, 0)))[0].astype(jnp.bfloat16)
    frames, height, columns, channels = latents.shape
    paired = doubled.reshape(frames, height, columns, 2, channels).transpose(0, 3, 1, 2, 4)
    return paired.reshape(2 * frames, height, columns, channels)
```

```python
import functools

import jax
import jax.numpy as jnp
from jax import lax
from jax.experimental import pallas as pl
from jax.experimental.pallas import tpu as pltpu
from jax.sharding import PartitionSpec as P

EPS = 1e-06
AXES = ("tm", "rows")
PAIRS = 16
BLOCKS = 8
PITCH = 112
CUT = 72


def device(pair, core, block):
    return (pair * 2 + core) * BLOCKS + block


def routes():
    every = [(m, c, r) for m in range(PAIRS) for c in range(2) for r in range(BLOCKS)]
    swap = [(device(m, c, r), device(m, 1 - c, r)) for m, c, r in every]
    ahead = [(device(m, c, r), device(m + 1, c, r)) for m, c, r in every if m + 1 < PAIRS]

    def back(m):
        return m // 4 * 4 + (m - 1) % 4

    behind = [(device(m, c, r), device(back(m), c, r)) for m, c, r in every if m + 2 < PAIRS]
    behind_again = [(device(back(m), c, r), device(m + 2, c, r)) for m, c, r in every if m + 2 < PAIRS]
    edges = []
    for m, c, r in every:
        to = r + (1 if c else -1)
        if 0 <= to < BLOCKS:
            edges.append((device(m, c, r), device(m, 1 - c, to)))
    return swap, ahead, behind, behind_again, edges


def send(block, route):
    return lax.ppermute(block, AXES, route)


def activate(values, gain):
    scaled = values * lax.rsqrt(jnp.mean(values * values, axis=-1, keepdims=True) + EPS) * gain
    return scaled / (1.0 + jnp.exp(-scaled))


def fill_taps(core, cells, outer, inner, gain, taps):
    rows, width, channels = cells.shape[1:]
    scale = gain[...]
    first = core == 0

    def frame(f, _):
        for q in range(rows + 2):
            if q == 0:
                values = jnp.where(first, outer[f, 0], inner[f, 0])
            elif q == rows + 1:
                values = jnp.where(first, inner[f, 0], outer[f, 0])
            else:
                values = cells[f, q - 1]
            active = activate(values.astype(jnp.float32), scale)
            active = jnp.concatenate([active, jnp.zeros((PITCH - width, channels), jnp.float32)], 0)
            columns = (pltpu.roll(active, 1, 0), active, pltpu.roll(active, PITCH - 1, 0))
            columns = [column.astype(jnp.bfloat16) for column in columns]
            for b in range(3):
                i = q - b
                if 0 <= i < rows:
                    for k in range(3):
                        start = (b * 3 + k) * channels
                        taps[f, i, :, start : start + channels] = columns[k]
        return 0

    lax.fori_loop(0, 2, frame, 0)


def product(taps, frames, weight):
    lhs = taps[frames]
    lhs = lhs.reshape(-1, lhs.shape[-1])
    return jnp.dot(lhs, weight, preferred_element_type=jnp.float32)


def late_terms(cells, taps, weight, total):
    rows, width, channels = cells.shape[1:]
    size = rows * PITCH
    both = product(taps, slice(0, 2), weight[2])
    total[...] = both.reshape(2, size, channels)
    for f in range(2):
        for i in range(rows):
            total[f, i * PITCH : i * PITCH + width] += cells[f, i].astype(jnp.float32)
    total[1] += product(taps, slice(0, 1), weight[1])


def early_terms(taps, weight):
    size = taps.shape[1] * PITCH
    both = product(taps, slice(0, 2), weight[0])
    more = product(taps, slice(1, 2), weight[1])
    return both[:size] + more, both[size:]


def stage_own(core, cells, outer, inner, gain, weight, total, taps):
    fill_taps(core[0], cells, outer, inner, gain, taps)
    late_terms(cells, taps, weight, total)


def stage_middle(core, cells, outer, inner, gain, weight, up, own, total, partial, taps):
    fill_taps(core[0], cells, outer, inner, gain, taps)
    terms = early_terms(taps, weight)
    first = (own[0] + terms[0]).astype(jnp.bfloat16)
    second = (own[1] + terms[1]).astype(jnp.bfloat16)
    dot = functools.partial(jnp.dot, preferred_element_type=jnp.float32)
    partial[0] = dot(first, up[2])
    partial[1] = dot(first, up[1]) + dot(second, up[2])
    late_terms(cells, taps, weight, total)


def stage_old(core, cells, outer, inner, gain, weight, up, own, partial, keep, give, taps):
    rows, width, channels = cells.shape[1:]
    fill_taps(core[0], cells, outer, inner, gain, taps)
    terms = early_terms(taps, weight)
    first = (own[0] + terms[0]).astype(jnp.bfloat16)
    second = (own[1] + terms[1]).astype(jnp.bfloat16)
    dot = functools.partial(jnp.dot, preferred_element_type=jnp.float32)
    even = partial[0] + dot(first, up[0]) + dot(second, up[1])
    odd = partial[1] + dot(second, up[0])

    def write(target, value):
        for k in range(2):
            for i in range(rows):
                piece = value[i * PITCH : i * PITCH + width, k * channels : (k + 1) * channels]
                target[k, i] = piece.astype(jnp.bfloat16)

    @pl.when(core[0] == 0)
    def _():
        write(keep, even)
        write(give, odd)

    @pl.when(core[0] != 0)
    def _():
        write(keep, odd)
        write(give, even)


def call(body, outs, flops, core, *args):
    rows, channels = args[0].shape[1], args[0].shape[3]
    whole = pl.BlockSpec(memory_space=pltpu.VMEM)
    return pl.pallas_call(
        body,
        out_shape=outs,
        in_specs=[pl.BlockSpec(memory_space=pltpu.SMEM)] + [whole] * len(args),
        out_specs=[whole] * len(outs),
        scratch_shapes=[pltpu.VMEM((2, rows, PITCH, 9 * channels), jnp.bfloat16)],
        compiler_params=pltpu.CompilerParams(vmem_limit_bytes=44 << 20),
        cost_estimate=pl.CostEstimate(flops=flops, bytes_accessed=10 << 20, transcendentals=0),
    )(core, *args)


def local(latents, norm_gain, conv_weight, up_weight):
    swap, ahead, behind, behind_again, edges = routes()
    core = lax.axis_index("tm") % 2
    rows, width, channels = latents.shape[1] // 2, latents.shape[2], latents.shape[3]
    gain = norm_gain.reshape(1, channels)
    weight = conv_weight.reshape(3, 9 * channels, channels)
    mark = core.reshape(1).astype(jnp.int32)
    size = rows * PITCH

    kept = lax.dynamic_slice_in_dim(latents, core * rows, rows, 1)
    given = lax.dynamic_slice_in_dim(latents, (1 - core) * rows, rows, 1)
    taken = send(given, swap)
    own = jnp.where(
        core == 0, jnp.concatenate([kept, taken], 0), jnp.concatenate([taken, kept], 0)
    )

    def borders(pair):
        outer = lax.dynamic_slice_in_dim(pair, core * (rows - 1), 1, 1)
        inner = lax.dynamic_slice_in_dim(pair, (1 - core) * (rows - 1), 1, 1)
        return send(outer, edges), send(inner, swap)

    middle = send(own, ahead)
    away = send(own[:, :, :CUT], behind)
    own_borders = borders(own)
    totals = jax.ShapeDtypeStruct((2, size, channels), jnp.float32)
    (own_total,) = call(stage_own, [totals], 10**10, mark, own, *own_borders, gain, weight)
    away = send(away, behind_again)
    near = send(middle[:, :, CUT:], ahead)
    middle_total, partial = call(
        stage_middle,
        [totals, jax.ShapeDtypeStruct((2, size, 2 * channels), jnp.float32)],
        2 * 10**10,
        mark,
        middle,
        *borders(middle),
        gain,
        weight,
        up_weight,
        own_total,
    )
    old = jnp.concatenate([away, near], 2)
    half = jax.ShapeDtypeStruct((2, rows, width, channels), jnp.bfloat16)
    keep, give = call(
        stage_old,
        [half, half],
        10**10,
        mark,
        old,
        *borders(old),
        gain,
        weight,
        up_weight,
        middle_total,
        partial,
    )
    got = send(give, swap)
    return jnp.where(
        core == 0, jnp.concatenate([keep, got], 1), jnp.concatenate([got, keep], 1)
    )


def solution(mesh):
    placed = (P("tm", "rows", None, None), P(), P(), P())
    return jax.shard_map(
        local, mesh=mesh, in_specs=placed, out_specs=P("tm", "rows", None, None), check_vma=False
    )
```

```python
import jax
import jax.numpy as jnp
from jax import lax
from jax.experimental import pallas as pl
from jax.experimental.pallas import tpu as pltpu
from jax.sharding import PartitionSpec as P

EPS = 1e-06
AXES = ("tm", "rows")
PAIRS = 16
BLOCKS = 8
PITCH = 112
CUT = 72


def device(pair, core, block):
    return (pair * 2 + core) * BLOCKS + block


def routes():
    every = [(m, c, r) for m in range(PAIRS) for c in range(2) for r in range(BLOCKS)]
    swap = [(device(m, c, r), device(m, 1 - c, r)) for m, c, r in every]
    ahead = [(device(m, c, r), device(m + 1, c, r)) for m, c, r in every if m + 1 < PAIRS]

    def back(m):
        return m // 4 * 4 + (m - 1) % 4

    far = [(m, c, r) for m, c, r in every if m + 2 < PAIRS]
    behind = [(device(m, c, r), device(back(m), c, r)) for m, c, r in far]
    behind_again = [(device(back(m), c, r), device(m + 2, c, r)) for m, c, r in far]
    edges = []
    for m, c, r in every:
        to = r + (1 if c else -1)
        if 0 <= to < BLOCKS:
            edges.append((device(m, c, r), device(m, 1 - c, to)))
    return swap, ahead, behind, behind_again, edges


def send(block, route):
    return lax.ppermute(block, AXES, route)


def dot(lhs, rhs):
    return jnp.dot(lhs, rhs, preferred_element_type=jnp.float32)


def columns_of(values, gain):
    values = values.astype(jnp.float32)
    scaled = values * lax.rsqrt(jnp.mean(values * values, axis=-1, keepdims=True) + EPS) * gain
    active = scaled / (1.0 + jnp.exp(-scaled))
    extra = jnp.zeros((PITCH - values.shape[0], values.shape[1]), jnp.float32)
    active = jnp.concatenate([active, extra], 0)
    shifts = (pltpu.roll(active, 1, 0), active, pltpu.roll(active, PITCH - 1, 0))
    return [shift.astype(jnp.bfloat16) for shift in shifts]


def fill_taps(row, gain, taps):
    rows, channels = taps.shape[1], taps.shape[3] // 9
    scale = gain[...]

    def frame(f, _):
        empty = [jnp.zeros((PITCH, channels), jnp.bfloat16)] * 3
        for q in range(rows + 2):
            inside = 0 < q <= rows
            columns = columns_of(row(f, q - 1), scale) if inside else empty
            for b in range(3):
                i = q - b
                if 0 <= i < rows:
                    for k in range(3):
                        start = (b * 3 + k) * channels
                        taps[f, i, :, start : start + channels] = columns[k]
        return 0

    lax.fori_loop(0, 2, frame, 0)


def product(taps, f, weight, *times):
    lhs = taps[f].reshape(-1, taps.shape[-1])
    return dot(lhs, jnp.concatenate([weight[a] for a in times], 1))


def late_terms(cells, taps, weight, total):
    rows, width, channels = cells.shape[1:]
    older = product(taps, 0, weight, 1, 2)
    total[0] = older[:, channels:]
    total[1] = older[:, :channels] + product(taps, 1, weight, 2)
    for f in range(2):
        for i in range(rows):
            total[f, i * PITCH : i * PITCH + width] += cells[f, i].astype(jnp.float32)


def early_terms(taps, weight, before, total):
    channels = weight.shape[2]
    newer = product(taps, 1, weight, 0, 1)
    total[1] = before[1] + newer[:, :channels]
    total[0] = before[0] + newer[:, channels:] + product(taps, 0, weight, 0)


def stage_own(cells, gain, source, total, weight, taps, done):
    copy = pltpu.make_async_copy(source, weight, done)
    copy.start()
    fill_taps(lambda f, i: cells[f, i], gain, taps)
    copy.wait()
    late_terms(cells, taps, weight, total)


def stage_middle(cells, gain, weight, own, own_total, total, taps):
    fill_taps(lambda f, i: cells[f, i], gain, taps)
    early_terms(taps, weight, own, own_total)
    late_terms(cells, taps, weight, total)


def stage_old(away, near, gain, weight, middle, total, taps):
    def row(f, i):
        return jnp.concatenate(
            [away[f, i].astype(jnp.float32), near[f, i].astype(jnp.float32)], 0
        )

    fill_taps(row, gain, taps)
    early_terms(taps, weight, middle, total)


def stage_last(
    core, outer, inner, outer_old, inner_old, gain, weight, up, own, middle, keep, give, edge, lines
):
    rows, width, channels = keep.shape[1:]
    scale = gain[...]
    first = core[0] == 0
    depth = 3 * channels

    def put(j, i, value):
        value = value.astype(jnp.bfloat16)
        for o in range(2):
            if 0 <= j - o < 3:
                start = (j - o) * channels
                lines[o, i * PITCH : (i + 1) * PITCH, start : start + channels] = value

    def total(j, i):
        return (middle, own)[j // 2][j % 2, i * PITCH : (i + 1) * PITCH]

    for j in range(4):
        for i in range(1, rows - 1):
            put(j, i, total(j, i))
    for top in (True, False):
        for frame in range(6):
            far, close = (outer_old, inner_old) if frame < 2 else (outer, inner)
            f = frame if frame < 2 else frame - 2
            pair = (far[f, 0], close[f, 0]) if top else (close[f, 0], far[f, 0])
            columns = columns_of(jnp.where(first, *pair), scale)
            for a in range(3):
                j = frame - a
                if 0 <= j < 4:
                    for k in range(3):
                        start = a * depth + k * channels
                        edge[j * PITCH : (j + 1) * PITCH, start : start + channels] = columns[k]
        b = 0 if top else 2
        part = [weight[a, b * depth : (b + 1) * depth] for a in range(3)]
        value = dot(edge[...], jnp.concatenate(part, 0))
        i = 0 if top else rows - 1
        for j in range(4):
            put(j, i, total(j, i) + value[j * PITCH : (j + 1) * PITCH])

    def write(target, value):
        for k in range(2):
            for i in range(rows):
                piece = value[i * PITCH : i * PITCH + width, k * channels : (k + 1) * channels]
                target[k, i] = piece.astype(jnp.bfloat16)

    even = dot(lines[0], up[...])
    odd = dot(lines[1], up[...])

    @pl.when(first)
    def _():
        write(keep, even)
        write(give, odd)

    @pl.when(jnp.logical_not(first))
    def _():
        write(keep, odd)
        write(give, even)


VMEM = pl.BlockSpec(memory_space=pltpu.VMEM)
SMEM = pl.BlockSpec(memory_space=pltpu.SMEM)
ANY = pl.BlockSpec(memory_space=pl.ANY)


def call(body, outs, flops, args, specs, scratch):
    return pl.pallas_call(
        body,
        out_shape=outs,
        in_specs=[specs.get(n, VMEM) for n in range(len(args))],
        out_specs=[VMEM] * len(outs),
        scratch_shapes=scratch,
        compiler_params=pltpu.CompilerParams(vmem_limit_bytes=32 << 20),
        cost_estimate=pl.CostEstimate(flops=flops, bytes_accessed=1 << 20, transcendentals=0),
    )(*args)


def local(latents, norm_gain, conv_weight, up_weight):
    swap, ahead, behind, behind_again, edges = routes()
    core = lax.axis_index("tm") % 2
    rows, width, channels = latents.shape[1] // 2, latents.shape[2], latents.shape[3]
    gain = norm_gain.reshape(1, channels)
    weight = conv_weight.reshape(3, 9 * channels, channels)
    up = up_weight.reshape(3 * channels, 2 * channels)
    mark = core.reshape(1).astype(jnp.int32)
    size = rows * PITCH
    taps = pltpu.VMEM((2, rows, PITCH, 9 * channels), jnp.bfloat16)
    totals = jax.ShapeDtypeStruct((2, size, channels), jnp.float32)
    half = jax.ShapeDtypeStruct((2, rows, width, channels), jnp.bfloat16)

    kept = lax.dynamic_slice_in_dim(latents, core * rows, rows, 1)
    given = lax.dynamic_slice_in_dim(latents, (1 - core) * rows, rows, 1)
    taken = send(given, swap)
    own = jnp.where(
        core == 0, jnp.concatenate([kept, taken], 0), jnp.concatenate([taken, kept], 0)
    )

    def outer(pair):
        return lax.dynamic_slice_in_dim(pair, core * (rows - 1), 1, 1)

    def inner(pair):
        return lax.dynamic_slice_in_dim(pair, (1 - core) * (rows - 1), 1, 1)

    middle = send(own, ahead)
    away = send(own[:, :, :CUT], behind)
    own_total, held = call(
        stage_own,
        [totals, jax.ShapeDtypeStruct(weight.shape, weight.dtype)],
        5 * 10**9,
        (own, gain, weight),
        {2: ANY},
        [taps, pltpu.SemaphoreType.DMA],
    )
    away, own_total = lax.optimization_barrier((away, own_total))
    away = send(away, behind_again)
    middle, own_total = lax.optimization_barrier((middle, own_total))
    both = jnp.concatenate([middle, own], 0)
    outer_near, inner_near = send(outer(both), edges), send(inner(both), swap)
    near = send(middle[:, :, CUT:], ahead)
    own_total, middle_total = call(
        stage_middle, [totals, totals], 10**10, (middle, gain, held, own_total), {}, [taps]
    )
    away, near, middle_total = lax.optimization_barrier((away, near, middle_total))

    def joined(pick):
        return jnp.concatenate([pick(away), pick(near)], 2)

    outer_old, inner_old = send(joined(outer), edges), send(joined(inner), swap)
    (middle_total,) = call(
        stage_old, [totals], 5 * 10**9, (away, near, gain, held, middle_total), {}, [taps]
    )
    keep, give = call(
        stage_last,
        [half, half],
        5 * 10**9,
        (mark, outer_near, inner_near, outer_old, inner_old, gain, held, up, own_total, middle_total),
        {0: SMEM},
        [
            pltpu.VMEM((size, 9 * channels), jnp.bfloat16),
            pltpu.VMEM((2, size, 3 * channels), jnp.bfloat16),
        ],
    )
    got = send(give, swap)
    return jnp.where(
        core == 0, jnp.concatenate([keep, got], 1), jnp.concatenate([got, keep], 1)
    )


def solution(mesh):
    placed = (P("tm", "rows", None, None), P(), P(), P())
    return jax.shard_map(
        local, mesh=mesh, in_specs=placed, out_specs=P("tm", "rows", None, None), check_vma=False
    )
```

```python
import jax
import jax.numpy as jnp
from jax import lax
from jax.experimental import pallas as pl
from jax.experimental.pallas import tpu as pltpu
from jax.sharding import PartitionSpec as P

EPS = 1e-06
AXES = ("tm", "rows")
PAIRS = 16
BLOCKS = 8
PITCH = 112
CUT = 64


def device(pair, core, block):
    return (pair * 2 + core) * BLOCKS + block


def routes():
    every = [(m, c, r) for m in range(PAIRS) for c in range(2) for r in range(BLOCKS)]
    swap = [(device(m, c, r), device(m, 1 - c, r)) for m, c, r in every]
    ahead = [(device(m, c, r), device(m + 1, c, r)) for m, c, r in every if m + 1 < PAIRS]

    def back(m):
        return m // 4 * 4 + (m - 1) % 4

    far = [(m, c, r) for m, c, r in every if m + 2 < PAIRS]
    behind = [(device(m, c, r), device(back(m), c, r)) for m, c, r in far]
    behind_again = [(device(back(m), c, r), device(m + 2, c, r)) for m, c, r in far]
    edges = []
    for m, c, r in every:
        to = r + (1 if c else -1)
        if 0 <= to < BLOCKS:
            edges.append((device(m, c, r), device(m, 1 - c, to)))
    return swap, ahead, behind, behind_again, edges


def send(block, route):
    return lax.ppermute(block, AXES, route)


def dot(lhs, rhs):
    return jnp.dot(lhs, rhs, preferred_element_type=jnp.float32)


def columns_of(values, gain):
    values = values.astype(jnp.float32)
    scaled = values * lax.rsqrt(jnp.mean(values * values, axis=-1, keepdims=True) + EPS) * gain
    active = scaled / (1.0 + jnp.exp(-scaled))
    extra = jnp.zeros((PITCH - values.shape[0], values.shape[1]), jnp.float32)
    active = jnp.concatenate([active, extra], 0)
    shifts = (pltpu.roll(active, 1, 0), active, pltpu.roll(active, PITCH - 1, 0))
    return [shift.astype(jnp.bfloat16) for shift in shifts]


def fill_taps(row, gain, taps):
    rows, channels = taps.shape[1], taps.shape[3] // 9
    scale = gain[...]

    def frame(f, _):
        empty = [jnp.zeros((PITCH, channels), jnp.bfloat16)] * 3
        for q in range(rows + 2):
            inside = 0 < q <= rows
            columns = columns_of(row(f, q - 1), scale) if inside else empty
            for b in range(3):
                i = q - b
                if 0 <= i < rows:
                    for k in range(3):
                        start = (b * 3 + k) * channels
                        taps[f, i, :, start : start + channels] = columns[k]
        return 0

    lax.fori_loop(0, 2, frame, 0)


def product(taps, f, weight, *times):
    lhs = taps[f].reshape(-1, taps.shape[-1])
    return dot(lhs, jnp.concatenate([weight[a] for a in times], 1))


def late_terms(cells, taps, weight, total):
    rows, width, channels = cells.shape[1:]
    older = product(taps, 0, weight, 1, 2)
    total[0] = older[:, channels:]
    total[1] = older[:, :channels] + product(taps, 1, weight, 2)
    for f in range(2):
        for i in range(rows):
            total[f, i * PITCH : i * PITCH + width] += cells[f, i].astype(jnp.float32)


def early_terms(taps, weight, before, total):
    channels = weight.shape[2]
    newer = product(taps, 1, weight, 0, 1)
    total[1] = before[1] + newer[:, :channels]
    total[0] = before[0] + newer[:, channels:] + product(taps, 0, weight, 0)


def stage_own(cells, gain, source, total, weight, taps, done):
    copy = pltpu.make_async_copy(source, weight, done)
    copy.start()
    fill_taps(lambda f, i: cells[f, i], gain, taps)
    copy.wait()
    late_terms(cells, taps, weight, total)


def stage_middle(cells, gain, weight, own, own_total, total, taps):
    fill_taps(lambda f, i: cells[f, i], gain, taps)
    early_terms(taps, weight, own, own_total)
    late_terms(cells, taps, weight, total)


def stage_old(away, near, gain, weight, middle, total, taps):
    def row(f, i):
        return jnp.concatenate(
            [away[f, i].astype(jnp.float32), near[f, i].astype(jnp.float32)], 0
        )

    fill_taps(row, gain, taps)
    early_terms(taps, weight, middle, total)


def stage_last(
    core, outer, inner, outer_old, inner_old, gain, weight, up, own, middle, keep, give, edge, lines
):
    rows, width, channels = keep.shape[1:]
    scale = gain[...]
    first = core[0] == 0
    depth = 3 * channels

    def put(j, i, value):
        value = value.astype(jnp.bfloat16)
        for o in range(2):
            if 0 <= j - o < 3:
                start = (j - o) * channels
                lines[o, i * PITCH : (i + 1) * PITCH, start : start + channels] = value

    def total(j, i):
        return (middle, own)[j // 2][j % 2, i * PITCH : (i + 1) * PITCH]

    for j in range(4):
        for i in range(1, rows - 1):
            put(j, i, total(j, i))
    for top in (True, False):
        for frame in range(6):
            far, close = (outer_old, inner_old) if frame < 2 else (outer, inner)
            f = frame if frame < 2 else frame - 2
            pair = (far[f, 0], close[f, 0]) if top else (close[f, 0], far[f, 0])
            columns = columns_of(jnp.where(first, *pair), scale)
            for a in range(3):
                j = frame - a
                if 0 <= j < 4:
                    for k in range(3):
                        start = a * depth + k * channels
                        edge[j * PITCH : (j + 1) * PITCH, start : start + channels] = columns[k]
        b = 0 if top else 2
        part = [weight[a, b * depth : (b + 1) * depth] for a in range(3)]
        value = dot(edge[...], jnp.concatenate(part, 0))
        i = 0 if top else rows - 1
        for j in range(4):
            put(j, i, total(j, i) + value[j * PITCH : (j + 1) * PITCH])

    def write(target, value):
        for k in range(2):
            for i in range(rows):
                piece = value[i * PITCH : i * PITCH + width, k * channels : (k + 1) * channels]
                target[k, i] = piece.astype(jnp.bfloat16)

    even = dot(lines[0], up[...])
    odd = dot(lines[1], up[...])

    @pl.when(first)
    def _():
        write(keep, even)
        write(give, odd)

    @pl.when(jnp.logical_not(first))
    def _():
        write(keep, odd)
        write(give, even)


VMEM = pl.BlockSpec(memory_space=pltpu.VMEM)
SMEM = pl.BlockSpec(memory_space=pltpu.SMEM)
ANY = pl.BlockSpec(memory_space=pl.ANY)


def call(body, outs, flops, args, specs, scratch):
    return pl.pallas_call(
        body,
        out_shape=outs,
        in_specs=[specs.get(n, VMEM) for n in range(len(args))],
        out_specs=[VMEM] * len(outs),
        scratch_shapes=scratch,
        compiler_params=pltpu.CompilerParams(vmem_limit_bytes=32 << 20),
        cost_estimate=pl.CostEstimate(flops=flops, bytes_accessed=1 << 20, transcendentals=0),
    )(*args)


def local(latents, norm_gain, conv_weight, up_weight):
    swap, ahead, behind, behind_again, edges = routes()
    core = lax.axis_index("tm") % 2
    rows, width, channels = latents.shape[1] // 2, latents.shape[2], latents.shape[3]
    gain = norm_gain.reshape(1, channels)
    weight = conv_weight.reshape(3, 9 * channels, channels)
    up = up_weight.reshape(3 * channels, 2 * channels)
    mark = core.reshape(1).astype(jnp.int32)
    size = rows * PITCH
    taps = pltpu.VMEM((2, rows, PITCH, 9 * channels), jnp.bfloat16)
    totals = jax.ShapeDtypeStruct((2, size, channels), jnp.float32)
    half = jax.ShapeDtypeStruct((2, rows, width, channels), jnp.bfloat16)

    kept = lax.dynamic_slice_in_dim(latents, core * rows, rows, 1)
    given = lax.dynamic_slice_in_dim(latents, (1 - core) * rows, rows, 1)
    taken = send(given, swap)
    own = jnp.where(
        core == 0, jnp.concatenate([kept, taken], 0), jnp.concatenate([taken, kept], 0)
    )

    def outer(pair):
        return lax.dynamic_slice_in_dim(pair, core * (rows - 1), 1, 1)

    def inner(pair):
        return lax.dynamic_slice_in_dim(pair, (1 - core) * (rows - 1), 1, 1)

    middle = send(own, ahead)
    away = send(own[:, :, :CUT], behind)
    own_total, held = call(
        stage_own,
        [totals, jax.ShapeDtypeStruct(weight.shape, weight.dtype)],
        5 * 10**9,
        (own, gain, weight),
        {2: ANY},
        [taps, pltpu.SemaphoreType.DMA],
    )
    away, own_total = lax.optimization_barrier((away, own_total))
    away = send(away, behind_again)
    middle, own_total = lax.optimization_barrier((middle, own_total))
    both = jnp.concatenate([middle, own], 0)
    outer_near, inner_near = send(outer(both), edges), send(inner(both), swap)
    near = send(middle[:, :, CUT:], ahead)
    own_total, middle_total = call(
        stage_middle, [totals, totals], 10**10, (middle, gain, held, own_total), {}, [taps]
    )
    away, near, middle_total = lax.optimization_barrier((away, near, middle_total))

    def joined(pick):
        return jnp.concatenate([pick(away), pick(near)], 2)

    outer_old, inner_old = send(joined(outer), edges), send(joined(inner), swap)
    (middle_total,) = call(
        stage_old, [totals], 5 * 10**9, (away, near, gain, held, middle_total), {}, [taps]
    )
    keep, give = call(
        stage_last,
        [half, half],
        5 * 10**9,
        (mark, outer_near, inner_near, outer_old, inner_old, gain, held, up, own_total, middle_total),
        {0: SMEM},
        [
            pltpu.VMEM((size, 9 * channels), jnp.bfloat16),
            pltpu.VMEM((2, size, 3 * channels), jnp.bfloat16),
        ],
    )
    got = send(give, swap)
    return jnp.where(
        core == 0, jnp.concatenate([keep, got], 1), jnp.concatenate([got, keep], 1)
    )


def solution(mesh):
    placed = (P("tm", "rows", None, None), P(), P(), P())
    return jax.shard_map(
        local, mesh=mesh, in_specs=placed, out_specs=P("tm", "rows", None, None), check_vma=False
    )
```

```python
import functools

import jax
import jax.numpy as jnp
from jax import lax
from jax.experimental import pallas as pl
from jax.experimental.pallas import tpu as pltpu
from jax.sharding import PartitionSpec as P

EPS = 1e-06
AXES = ("tm", "rows")
PAIRS = 16
BLOCKS = 8
PITCH = 112
CUT = 16


def device(pair, core, block):
    return (pair * 2 + core) * BLOCKS + block


def routes():
    every = [(m, c, r) for m in range(PAIRS) for c in range(2) for r in range(BLOCKS)]
    swap = [(device(m, c, r), device(m, 1 - c, r)) for m, c, r in every]
    near = [(m, c, r) for m, c, r in every if m + 1 < PAIRS]
    ahead = [(device(m, c, r), device(m + 1, c, r)) for m, c, r in near]
    crossed = [(device(m, c, r), device(m + 1, 1 - c, r)) for m, c, r in near]

    def back(m):
        return m // 4 * 4 + (m - 1) % 4

    far = [(m, c, r) for m, c, r in every if m + 2 < PAIRS]
    behind = [(device(m, c, r), device(back(m), c, r)) for m, c, r in far]
    behind_again = [(device(back(m), c, r), device(m + 2, c, r)) for m, c, r in far]
    edges = []
    for m, c, r in every:
        to = r + (1 if c else -1)
        if 0 <= to < BLOCKS:
            edges.append((device(m, c, r), device(m, 1 - c, to)))
    return swap, ahead, crossed, behind, behind_again, edges


def send(block, route):
    return lax.ppermute(block, AXES, route)


def dot(lhs, rhs):
    return jnp.dot(lhs, rhs, preferred_element_type=jnp.float32)


def columns_of(values, gain):
    values = values.astype(jnp.float32)
    scaled = values * lax.rsqrt(jnp.mean(values * values, axis=-1, keepdims=True) + EPS) * gain
    active = scaled / (1.0 + jnp.exp(-scaled))
    extra = jnp.zeros((PITCH - values.shape[0], values.shape[1]), jnp.float32)
    active = jnp.concatenate([active, extra], 0)
    shifts = (pltpu.roll(active, 1, 0), active, pltpu.roll(active, PITCH - 1, 0))
    return [shift.astype(jnp.bfloat16) for shift in shifts]


def fill_taps(row, gain, taps):
    rows, channels = taps.shape[0], taps.shape[2] // 9
    scale = gain[...]
    empty = [jnp.zeros((PITCH, channels), jnp.bfloat16)] * 3
    for q in range(rows + 2):
        columns = columns_of(row(q - 1), scale) if 0 < q <= rows else empty
        for b in range(3):
            i = q - b
            if 0 <= i < rows:
                for k in range(3):
                    start = (b * 3 + k) * channels
                    taps[i, :, start : start + channels] = columns[k]


def product(taps, weight, *times):
    lhs = taps[...].reshape(-1, taps.shape[-1])
    return dot(lhs, jnp.concatenate([weight[a] for a in times], 1))


def stage_own(core, same, cross, gain, source, total, weight, taps, done):
    rows, width, channels = same.shape[1:]
    copy = pltpu.make_async_copy(source, weight, done)
    copy.start()

    def row(f, i):
        return jnp.where(core[0] == f, same[0, i], cross[0, i])

    def fill(f, _):
        fill_taps(functools.partial(row, f), gain, taps.at[f])
        return 0

    lax.fori_loop(0, 2, fill, 0)
    total[0] = jnp.zeros(total.shape[1:], jnp.float32)
    total[1] = jnp.zeros(total.shape[1:], jnp.float32)
    copy.wait()
    older = product(taps.at[0], weight, 1, 2)
    total[2] = older[:, channels:]
    total[3] = older[:, :channels] + product(taps.at[1], weight, 2)
    for f in range(2):
        for i in range(rows):
            total[2 + f, i * PITCH : i * PITCH + width] += row(f, i).astype(jnp.float32)


def stage_frame(crossing, core, cells, gain, weight, before, total, taps):
    rows, width, channels = cells.shape[1:]
    frame = 3 - core[0] if crossing else 2 + core[0]
    fill_taps(lambda i: cells[0, i], gain, taps)
    terms = product(taps, weight, 0, 1, 2)
    rest = jnp.where(frame == 3, 0, 3)
    total[rest] = before[rest]
    for a in range(3):
        total[frame - a] = before[frame - a] + terms[:, a * channels : (a + 1) * channels]
    for i in range(rows):
        area = pl.ds(i * PITCH, width)
        total[frame - 2, area] += cells[0, i].astype(jnp.float32)


def stage_old(core, away, near, gain, weight, before, total, taps):
    rows, width, channels = away.shape[1], near.shape[2] + CUT, away.shape[3]

    def row(f, i):
        start = away[0, i, :CUT].astype(jnp.float32)
        same = jnp.concatenate([start, near[0, i].astype(jnp.float32)], 0)
        return jnp.where(core[0] == f, same, away[0, i, CUT:].astype(jnp.float32))

    def fill(f, _):
        fill_taps(functools.partial(row, f), gain, taps.at[f])
        return 0

    lax.fori_loop(0, 2, fill, 0)
    newer = product(taps.at[1], weight, 0, 1)
    total[1] = before[1] + newer[:, :channels]
    total[0] = before[0] + newer[:, channels:] + product(taps.at[0], weight, 0)
    total[2] = before[2]
    total[3] = before[3]


def stage_last(
    core, outer, inner, outer_old, inner_old, gain, weight, up, sums, keep, give, edge, lines
):
    rows, width, channels = keep.shape[1:]
    scale = gain[...]
    first = core[0] == 0
    depth = 3 * channels

    def put(j, i, value):
        value = value.astype(jnp.bfloat16)
        for o in range(2):
            if 0 <= j - o < 3:
                start = (j - o) * channels
                lines[o, i * PITCH : (i + 1) * PITCH, start : start + channels] = value

    def border(frame, top):
        far, close = (outer, inner), (outer_old, inner_old)
        same, cross = (
            ((close, 1), (close, 2)),
            ((far, 2), (close, 0)),
            ((far, 0), (far, 1)),
        )[frame // 2]
        zero, one = (same, cross) if frame % 2 else (cross, same)
        at_zero = zero[0][0 if top else 1][zero[1], 0]
        at_one = one[0][1 if top else 0][one[1], 0]
        return jnp.where(first, at_zero, at_one)

    for j in range(4):
        for i in range(1, rows - 1):
            put(j, i, sums[j, i * PITCH : (i + 1) * PITCH])
    for top in (True, False):
        for frame in range(6):
            columns = columns_of(border(frame, top), scale)
            for a in range(3):
                j = frame - a
                if 0 <= j < 4:
                    for k in range(3):
                        start = a * depth + k * channels
                        edge[j * PITCH : (j + 1) * PITCH, start : start + channels] = columns[k]
        b = 0 if top else 2
        part = [weight[a, b * depth : (b + 1) * depth] for a in range(3)]
        value = dot(edge[...], jnp.concatenate(part, 0))
        i = 0 if top else rows - 1
        for j in range(4):
            area = slice(j * PITCH, (j + 1) * PITCH)
            put(j, i, sums[j, i * PITCH : (i + 1) * PITCH] + value[area])

    def write(target, value):
        for k in range(2):
            for i in range(rows):
                piece = value[i * PITCH : i * PITCH + width, k * channels : (k + 1) * channels]
                target[k, i] = piece.astype(jnp.bfloat16)

    even = dot(lines[0], up[...])
    odd = dot(lines[1], up[...])

    @pl.when(first)
    def _():
        write(keep, even)
        write(give, odd)

    @pl.when(jnp.logical_not(first))
    def _():
        write(keep, odd)
        write(give, even)


VMEM = pl.BlockSpec(memory_space=pltpu.VMEM)
SMEM = pl.BlockSpec(memory_space=pltpu.SMEM)
ANY = pl.BlockSpec(memory_space=pl.ANY)


def call(body, outs, flops, args, scratch, specs=(), limit=26):
    specs = {0: SMEM, **dict(specs)}
    return pl.pallas_call(
        body,
        out_shape=outs,
        in_specs=[specs.get(n, VMEM) for n in range(len(args))],
        out_specs=[VMEM] * len(outs),
        scratch_shapes=scratch,
        compiler_params=pltpu.CompilerParams(vmem_limit_bytes=limit << 20),
        cost_estimate=pl.CostEstimate(flops=flops, bytes_accessed=1 << 20, transcendentals=0),
    )(*args)


def local(latents, norm_gain, conv_weight, up_weight):
    swap, ahead, crossed, behind, behind_again, edges = routes()
    core = lax.axis_index("tm") % 2
    rows, width, channels = latents.shape[1] // 2, latents.shape[2], latents.shape[3]
    gain = norm_gain.reshape(1, channels)
    source = conv_weight.reshape(3, 9 * channels, channels)
    up = up_weight.reshape(3 * channels, 2 * channels)
    mark = core.reshape(1).astype(jnp.int32)
    size = rows * PITCH
    taps = pltpu.VMEM((rows, PITCH, 9 * channels), jnp.bfloat16)
    pair = pltpu.VMEM((2, rows, PITCH, 9 * channels), jnp.bfloat16)
    totals = jax.ShapeDtypeStruct((4, size, channels), jnp.float32)
    half = jax.ShapeDtypeStruct((2, rows, width, channels), jnp.bfloat16)

    def borders(*frames):
        block = jnp.concatenate(frames, 0)
        outer = lax.dynamic_slice_in_dim(block, core * (rows - 1), 1, 1)
        inner = lax.dynamic_slice_in_dim(block, (1 - core) * (rows - 1), 1, 1)
        return send(outer, edges), send(inner, swap)

    kept = lax.dynamic_slice_in_dim(latents, core * rows, rows, 1)
    given = lax.dynamic_slice_in_dim(latents, (1 - core) * rows, rows, 1)
    same = send(kept, ahead)
    taken = send(given, swap)
    given, taken = lax.optimization_barrier((given, taken))
    cross = send(given, crossed)
    away = send(jnp.concatenate([kept[:, :, :CUT], taken], 2), behind)
    total, weight = call(
        stage_own,
        [totals, jax.ShapeDtypeStruct(source.shape, source.dtype)],
        5 * 10**9,
        (mark, kept, taken, gain, source),
        [pair, pltpu.SemaphoreType.DMA],
        {4: ANY},
        limit=46,
    )
    same, total = lax.optimization_barrier((same, total))
    near = send(same[:, :, CUT:], ahead)
    same, away, total = lax.optimization_barrier((same, away, total))
    away = send(away, behind_again)
    near_borders = borders(kept, taken, same)
    (total,) = call(
        functools.partial(stage_frame, False),
        [totals],
        10**9,
        (mark, same, gain, weight, total),
        [taps],
    )
    cross, total = lax.optimization_barrier((cross, total))
    (total,) = call(
        functools.partial(stage_frame, True),
        [totals],
        10**9,
        (mark, cross, gain, weight, total),
        [taps],
    )
    away, near, total = lax.optimization_barrier((away, near, total))
    old = jnp.concatenate([away[:, :, :CUT], near], 2)
    old_borders = borders(cross, old, away[:, :, CUT:])
    (total,) = call(
        stage_old, [totals], 5 * 10**9, (mark, away, near, gain, weight, total), [pair]
    )
    keep, give = call(
        stage_last,
        [half, half],
        5 * 10**9,
        (mark, *near_borders, *old_borders, gain, weight, up, total),
        [
            pltpu.VMEM((size, 9 * channels), jnp.bfloat16),
            pltpu.VMEM((2, size, 3 * channels), jnp.bfloat16),
        ],
    )
    got = send(give, swap)
    return jnp.where(
        core == 0, jnp.concatenate([keep, got], 1), jnp.concatenate([got, keep], 1)
    )


def solution(mesh):
    placed = (P("tm", "rows", None, None), P(), P(), P())
    return jax.shard_map(
        local, mesh=mesh, in_specs=placed, out_specs=P("tm", "rows", None, None), check_vma=False
    )
```

```python
import jax
import jax.numpy as jnp
from jax import lax
from jax.experimental import pallas as pl
from jax.experimental.pallas import tpu as pltpu
from jax.sharding import PartitionSpec as P

EPS = 1e-06
AXES = ("tm", "rows")
PAIRS = 16
BLOCKS = 8
PITCH = 112
CUT = 64


def device(pair, core, block):
    return (pair * 2 + core) * BLOCKS + block


def routes():
    every = [(m, c, r) for m in range(PAIRS) for c in range(2) for r in range(BLOCKS)]
    swap = [(device(m, c, r), device(m, 1 - c, r)) for m, c, r in every]
    ahead = [(device(m, c, r), device(m + 1, c, r)) for m, c, r in every if m + 1 < PAIRS]

    def back(m):
        return m // 4 * 4 + (m - 1) % 4

    far = [(m, c, r) for m, c, r in every if m + 2 < PAIRS]
    behind = [(device(m, c, r), device(back(m), c, r)) for m, c, r in far]
    behind_again = [(device(back(m), c, r), device(m + 2, c, r)) for m, c, r in far]
    edges = []
    for m, c, r in every:
        to = r + (1 if c else -1)
        if 0 <= to < BLOCKS:
            edges.append((device(m, c, r), device(m, 1 - c, to)))
    return swap, ahead, behind, behind_again, edges


def send(block, route):
    return lax.ppermute(block, AXES, route)


def dot(lhs, rhs):
    return jnp.dot(lhs, rhs, preferred_element_type=jnp.float32)


def columns_of(values, gain):
    values = values.astype(jnp.float32)
    scaled = values * lax.rsqrt(jnp.mean(values * values, axis=-1, keepdims=True) + EPS) * gain
    active = scaled / (1.0 + jnp.exp(-scaled))
    extra = jnp.zeros((PITCH - values.shape[0], values.shape[1]), jnp.float32)
    active = jnp.concatenate([active, extra], 0)
    shifts = (pltpu.roll(active, 1, 0), active, pltpu.roll(active, PITCH - 1, 0))
    return [shift.astype(jnp.bfloat16) for shift in shifts]


def fill_taps(row, gain, taps):
    rows, channels = taps.shape[1], taps.shape[3] // 9
    scale = gain[...]

    def frame(f, _):
        empty = [jnp.zeros((PITCH, channels), jnp.bfloat16)] * 3
        for q in range(rows + 2):
            inside = 0 < q <= rows
            columns = columns_of(row(f, q - 1), scale) if inside else empty
            for b in range(3):
                i = q - b
                if 0 <= i < rows:
                    for k in range(3):
                        start = (b * 3 + k) * channels
                        taps[f, i, :, start : start + channels] = columns[k]
        return 0

    lax.fori_loop(0, 2, frame, 0)


def product(taps, f, weight, *times):
    lhs = taps[f].reshape(-1, taps.shape[-1])
    return dot(lhs, jnp.concatenate([weight[a] for a in times], 1))


def late_terms(cells, taps, weight, total):
    rows, width, channels = cells.shape[1:]
    older = product(taps, 0, weight, 1, 2)
    total[0] = older[:, channels:]
    total[1] = older[:, :channels] + product(taps, 1, weight, 2)
    for f in range(2):
        for i in range(rows):
            total[f, i * PITCH : i * PITCH + width] += cells[f, i].astype(jnp.float32)


def early_terms(taps, weight, before, total):
    channels = weight.shape[2]
    newer = product(taps, 1, weight, 0, 1)
    total[1] = before[1] + newer[:, :channels]
    total[0] = before[0] + newer[:, channels:] + product(taps, 0, weight, 0)


def stage_own(cells, gain, source, total, weight, taps, done):
    copy = pltpu.make_async_copy(source, weight, done)
    copy.start()
    fill_taps(lambda f, i: cells[f, i], gain, taps)
    copy.wait()
    late_terms(cells, taps, weight, total)


def stage_middle(cells, gain, weight, own, own_total, total, taps):
    fill_taps(lambda f, i: cells[f, i], gain, taps)
    early_terms(taps, weight, own, own_total)
    late_terms(cells, taps, weight, total)


def stage_old(away, near, gain, weight, middle, total, taps):
    def row(f, i):
        return jnp.concatenate(
            [away[f, i].astype(jnp.float32), near[f, i].astype(jnp.float32)], 0
        )

    fill_taps(row, gain, taps)
    early_terms(taps, weight, middle, total)


def stage_last(
    core, outer, inner, outer_old, inner_old, gain, weight, up, own, middle, give, lines, edge
):
    rows, width, channels = give.shape[1:]
    scale = gain[...]
    first = core[0] == 0
    depth = 3 * channels

    def put(j, i, value):
        value = value.astype(jnp.bfloat16)
        for o in range(2):
            if 0 <= j - o < 3:
                start = (j - o) * channels
                lines[o, i * PITCH : (i + 1) * PITCH, start : start + channels] = value

    def total(j, i):
        return (middle, own)[j // 2][j % 2, i * PITCH : (i + 1) * PITCH]

    for j in range(4):
        for i in range(1, rows - 1):
            put(j, i, total(j, i))
    for top in (True, False):
        for frame in range(6):
            far, close = (outer_old, inner_old) if frame < 2 else (outer, inner)
            f = frame if frame < 2 else frame - 2
            pair = (far[f, 0], close[f, 0]) if top else (close[f, 0], far[f, 0])
            columns = columns_of(jnp.where(first, *pair), scale)
            for a in range(3):
                j = frame - a
                if 0 <= j < 4:
                    for k in range(3):
                        start = a * depth + k * channels
                        edge[j * PITCH : (j + 1) * PITCH, start : start + channels] = columns[k]
        b = 0 if top else 2
        part = [weight[a, b * depth : (b + 1) * depth] for a in range(3)]
        value = dot(edge[...], jnp.concatenate(part, 0))
        i = 0 if top else rows - 1
        for j in range(4):
            put(j, i, total(j, i) + value[j * PITCH : (j + 1) * PITCH])

    write(give, dot(lines[1 - core[0]], up[...]))


def write(target, value):
    rows, width, channels = target.shape[1:]
    for k in range(2):
        for i in range(rows):
            piece = value[i * PITCH : i * PITCH + width, k * channels : (k + 1) * channels]
            target[k, i] = piece.astype(jnp.bfloat16)


def stage_keep(core, lines, up, keep):
    write(keep, dot(lines[core[0]], up[...]))


VMEM = pl.BlockSpec(memory_space=pltpu.VMEM)
SMEM = pl.BlockSpec(memory_space=pltpu.SMEM)
ANY = pl.BlockSpec(memory_space=pl.ANY)


def call(body, outs, flops, args, specs, scratch):
    return pl.pallas_call(
        body,
        out_shape=outs,
        in_specs=[specs.get(n, VMEM) for n in range(len(args))],
        out_specs=[VMEM] * len(outs),
        scratch_shapes=scratch,
        compiler_params=pltpu.CompilerParams(vmem_limit_bytes=32 << 20),
        cost_estimate=pl.CostEstimate(flops=flops, bytes_accessed=1 << 20, transcendentals=0),
    )(*args)


def local(latents, norm_gain, conv_weight, up_weight):
    swap, ahead, behind, behind_again, edges = routes()
    core = lax.axis_index("tm") % 2
    rows, width, channels = latents.shape[1] // 2, latents.shape[2], latents.shape[3]
    gain = norm_gain.reshape(1, channels)
    weight = conv_weight.reshape(3, 9 * channels, channels)
    up = up_weight.reshape(3 * channels, 2 * channels)
    mark = core.reshape(1).astype(jnp.int32)
    size = rows * PITCH
    taps = pltpu.VMEM((2, rows, PITCH, 9 * channels), jnp.bfloat16)
    totals = jax.ShapeDtypeStruct((2, size, channels), jnp.float32)
    half = jax.ShapeDtypeStruct((2, rows, width, channels), jnp.bfloat16)

    kept = lax.dynamic_slice_in_dim(latents, core * rows, rows, 1)
    given = lax.dynamic_slice_in_dim(latents, (1 - core) * rows, rows, 1)
    taken = send(given, swap)
    own = jnp.where(
        core == 0, jnp.concatenate([kept, taken], 0), jnp.concatenate([taken, kept], 0)
    )

    def outer(pair):
        return lax.dynamic_slice_in_dim(pair, core * (rows - 1), 1, 1)

    def inner(pair):
        return lax.dynamic_slice_in_dim(pair, (1 - core) * (rows - 1), 1, 1)

    middle = send(own, ahead)
    away = send(own[:, :, :CUT], behind)
    own_total, held = call(
        stage_own,
        [totals, jax.ShapeDtypeStruct(weight.shape, weight.dtype)],
        5 * 10**9,
        (own, gain, weight),
        {2: ANY},
        [taps, pltpu.SemaphoreType.DMA],
    )
    away, own_total = lax.optimization_barrier((away, own_total))
    away = send(away, behind_again)
    middle, own_total = lax.optimization_barrier((middle, own_total))
    both = jnp.concatenate([middle, own], 0)
    outer_near, inner_near = send(outer(both), edges), send(inner(both), swap)
    near = send(middle[:, :, CUT:], ahead)
    own_total, middle_total = call(
        stage_middle, [totals, totals], 10**10, (middle, gain, held, own_total), {}, [taps]
    )
    away, near, middle_total = lax.optimization_barrier((away, near, middle_total))

    def joined(pick):
        return jnp.concatenate([pick(away), pick(near)], 2)

    outer_old, inner_old = send(joined(outer), edges), send(joined(inner), swap)
    (middle_total,) = call(
        stage_old, [totals], 5 * 10**9, (away, near, gain, held, middle_total), {}, [taps]
    )
    give, lines = call(
        stage_last,
        [half, jax.ShapeDtypeStruct((2, size, 3 * channels), jnp.bfloat16)],
        5 * 10**9,
        (mark, outer_near, inner_near, outer_old, inner_old, gain, held, up, own_total, middle_total),
        {0: SMEM},
        [
            pltpu.VMEM((size, 9 * channels), jnp.bfloat16),
        ],
    )
    got = send(give, swap)
    (keep,) = call(stage_keep, [half], 10**9, (mark, lines, up), {0: SMEM}, [])
    return jnp.where(
        core == 0, jnp.concatenate([keep, got], 1), jnp.concatenate([got, keep], 1)
    )


def solution(mesh):
    placed = (P("tm", "rows", None, None), P(), P(), P())
    return jax.shard_map(
        local, mesh=mesh, in_specs=placed, out_specs=P("tm", "rows", None, None), check_vma=False
    )
```
